32 devices in a mesh: lat: 8 (over z, y), slot: 4 (over x, core).
Axes of the slice: x: 2, y: 2, z: 4, core: 2. Of those that a mesh axis runs over, the one named last changes fastest.
Arguments:
- seasonal_normals: bfloat16 [64, 8, 704, 1440], P('slot', None, 'lat'), may hold values from -24 to 24
- overlay_coarse_parallels: int32 [128, 10], P('lat'), may hold values from 0 to 703, as said below
- overlay_extent_factor: float32 [128, 10], P('lat'), may hold values from 0.2 to 1
- overlay_member_number: int32 [128], P('lat'), may hold values from 7 to 10
- verifying_seasonal_bin: int32 [128, 4], P('slot'), may hold values from 0 to 63
- prognosis_grid: bfloat16 [128, 4, 8, 128, 240], P('slot', None, None, 'lat'), may hold values from -6 to 6
- observed_analysis: bfloat16 [128, 4, 8, 128, 240], P('slot', None, None, 'lat'), may hold values from -6 to 6
Outputs:
- rmse_map: float32 [4, 8, 128, 240], P('slot', None, 'lat')
- acc_map: float32 [4, 8, 128, 240], P('slot', None, 'lat')
The draws below stay inside these ranges and needn't reach their ends.
Inputs may be any that keep to these rules, and one draw needn't show every extreme that they name: `overlay_coarse_parallels`: for k < overlay_member_number[t] the entries of row t are the consecutive source rows that target row t margins; later entries are padding and repeat live entries. With center(t) = ((2t + 1) * 704) // 256, every entry of row t lies in source rows max(center(t) - 5, 0) to min(center(t) + 4, 703).
All inputs are finite; a program needn't handle non-finite values.
Results may differ from the reference program's by a relative error of at most 0.00085.
Values may be sent and summed in bfloat16 or wider, within the bound.
A program may use at most 256 MiB of HBM per device.

```python
import math
import jax
import jax.numpy as jnp
from jax import lax

SRC_LAT = 704
SRC_LON = 1440
DEST_PARALLELS = 128
DEST_MERIDIANS = 240
NUM_VARIABLES = 8
SEASONAL_BINS = 64
HORIZON_STEPS = 4
OVER = 10
INIT_DAYS = 128
TGT_TILE = 16


def margin_lists(key):
    target = jnp.arange(DEST_PARALLELS, dtype=jnp.int32)
    center = (2 * target + 1) * SRC_LAT // (2 * DEST_PARALLELS)
    below = jax.random.randint(jax.random.fold_in(key, 11), (DEST_PARALLELS,), 3, 6, dtype=jnp.int32)
    above = jax.random.randint(jax.random.fold_in(key, 12), (DEST_PARALLELS,), 3, 5, dtype=jnp.int32)
    below = jnp.where(target % TGT_TILE == 0, 5, below)
    above = jnp.where(target % TGT_TILE == TGT_TILE - 1, 4, above)
    first_row = jnp.maximum(center - below, 0)
    final_row = jnp.minimum(center + above, SRC_LAT - 1)
    final_row = jnp.minimum(jnp.maximum(final_row, first_row + 6), SRC_LAT - 1)
    first_row = jnp.maximum(jnp.minimum(first_row, final_row - 6), 0)
    length = final_row - first_row + 1
    entries = jnp.arange(OVER, dtype=jnp.int32)
    filler = jax.random.randint(jax.random.fold_in(key, 13), (DEST_PARALLELS, OVER), 0, 1 << 20, dtype=jnp.int32) % length[:, None]
    offset = jnp.where(entries[None, :] < length[:, None], entries[None, :], filler)
    source_rows = jnp.clip(first_row[:, None] + offset, 0, SRC_LAT - 1)
    return (source_rows.astype(jnp.int32), length.astype(jnp.int32))


def draw_overlay_coarse_parallels(key, part):
    return margin_lists(jax.random.fold_in(key, 7))[0]


def draw_overlay_member_number(key, part):
    return margin_lists(jax.random.fold_in(key, 7))[1]


def set_ends(result, rng, low, top_value):
    longest = result.shape.index(max(result.shape))
    spots = []
    for shift in (0, 1):
        where = [jax.random.randint(jax.random.fold_in(rng, axis), (), 0, length) for axis, length in enumerate(result.shape)]
        where[longest] = (where[longest] + shift) % result.shape[longest]
        spots.append(tuple(where))
    return result.at[spots[0]].set(low).at[spots[1]].set(top_value)


def steps_of(own_key, shape, pieces, least, top_value):
    factor_of, own = 1.0, jax.random.fold_in(own_key, 6)
    for axis_at, parts in pieces:
        draws = jnp.exp(jax.random.uniform(jax.random.fold_in(own, axis_at), (parts,), jnp.float32, least / len(pieces), top_value / len(pieces)))
        factor_of = factor_of * jnp.repeat(draws, shape[axis_at] // parts).reshape([-1 if axis == axis_at else 1 for axis in range(len(shape))])
    return factor_of


def normal_values(own_key, extent, spread, reach, pieces=(), held_as=jnp.bfloat16):
    array = jax.random.normal(own_key, extent, jnp.float32) * spread
    if len(pieces) > 0:
        array = steps_of(own_key, extent, pieces, -0.22, 0.18) * array
    return jnp.clip(array, min=-reach, max=reach).astype(held_as)


def setup_inputs(seed: int = 0) -> dict:
    key_of = jax.random.split(jax.random.key(seed), 8)
    seasonal_normals = normal_values(key_of[0], (SEASONAL_BINS, NUM_VARIABLES, SRC_LAT, SRC_LON), 4.0, 24.0, ((0, 4), (2, 8)))
    overlay_coarse_parallels = draw_overlay_coarse_parallels(jax.random.fold_in(key_of[7], 71), 0)
    overlay_extent_factor = jnp.clip(0.2 + 0.8 * jax.random.uniform(key_of[2], (DEST_PARALLELS, OVER), jnp.float32) ** steps_of(key_of[2], (DEST_PARALLELS, OVER), ((0, 8),), -0.2, 0.2), 0.2, 1.0)
    overlay_member_number = draw_overlay_member_number(jax.random.fold_in(key_of[7], 71), 0)
    verifying_seasonal_bin = set_ends(jax.random.randint(key_of[4], (INIT_DAYS, HORIZON_STEPS), 0, SEASONAL_BINS), jax.random.fold_in(key_of[4], 1), 0, SEASONAL_BINS - 1).astype(jnp.int32)
    prognosis_grid = normal_values(key_of[5], (INIT_DAYS, HORIZON_STEPS, NUM_VARIABLES, DEST_PARALLELS, DEST_MERIDIANS), 1.0, 6.0, ((0, 4), (3, 8)))
    observed_analysis = normal_values(key_of[6], (INIT_DAYS, HORIZON_STEPS, NUM_VARIABLES, DEST_PARALLELS, DEST_MERIDIANS), 1.0, 6.0, ((0, 4), (3, 8)))
    return dict(seasonal_normals=seasonal_normals, overlay_coarse_parallels=overlay_coarse_parallels, overlay_extent_factor=overlay_extent_factor, overlay_member_number=overlay_member_number, verifying_seasonal_bin=verifying_seasonal_bin, prognosis_grid=prognosis_grid, observed_analysis=observed_analysis)


def reference(seasonal_normals, overlay_coarse_parallels, overlay_extent_factor, overlay_member_number, verifying_seasonal_bin, prognosis_grid, observed_analysis):
    meridian_refinement = SRC_LON // DEST_MERIDIANS
    lon_mean = (lax.optimization_barrier(jnp.sum(seasonal_normals.reshape(SEASONAL_BINS, NUM_VARIABLES, SRC_LAT, DEST_MERIDIANS, meridian_refinement), axis=-1, dtype=jnp.float32)) * (1.0 / meridian_refinement)).astype(jnp.bfloat16)
    live_slots = jnp.arange(OVER, dtype=jnp.int32)[None, :] < overlay_member_number[:, None]
    raw_weight = jnp.where(live_slots, overlay_extent_factor, jnp.zeros_like(overlay_extent_factor))
    weight = raw_weight / lax.optimization_barrier(jnp.sum(raw_weight, axis=1, keepdims=True))
    climate = jnp.zeros((SEASONAL_BINS, NUM_VARIABLES, DEST_PARALLELS, DEST_MERIDIANS), jnp.float32)
    for entry in range(OVER):
        picked = jnp.take(lon_mean, overlay_coarse_parallels[:, entry].astype(jnp.int32), axis=2).astype(jnp.float32)
        climate = climate + weight[:, entry][None, None, :, None] * picked
    latitude = (jnp.arange(DEST_PARALLELS, dtype=jnp.float32) + 0.5) * (math.pi / DEST_PARALLELS) - 0.5 * math.pi
    cosine = jnp.cos(latitude)
    parallel_cosine_factor = cosine / jnp.mean(cosine)
    misfit_spread_record = []
    acc_list = []
    for horizon_position in range(HORIZON_STEPS):
        clim_valid = jnp.take(climate, verifying_seasonal_bin[:, horizon_position].astype(jnp.int32), axis=0)
        prognosis_snapshot = prognosis_grid[:, horizon_position].astype(jnp.float32)
        observed = observed_analysis[:, horizon_position].astype(jnp.float32)
        error = prognosis_snapshot - observed
        fore_anom = prognosis_snapshot - clim_valid
        true_anom = observed - clim_valid
        squared_misfit = lax.optimization_barrier(jnp.sum(error * error, axis=0))
        cross_sum = lax.optimization_barrier(jnp.sum(fore_anom * true_anom, axis=0))
        fore_sq = lax.optimization_barrier(jnp.sum(fore_anom * fore_anom, axis=0))
        true_sq = lax.optimization_barrier(jnp.sum(true_anom * true_anom, axis=0))
        misfit_spread_record.append(jnp.sqrt(parallel_cosine_factor[None, :, None] * squared_misfit / INIT_DAYS))
        acc_list.append(cross_sum / jnp.sqrt(fore_sq * true_sq + 1e-06))
    return (jnp.stack(misfit_spread_record, axis=0), jnp.stack(acc_list, axis=0))
```

```python
import math
import functools

import jax
import jax.numpy as jnp
from jax import lax
from jax.experimental import pallas as pl
from jax.experimental.pallas import tpu as pltpu
from jax.sharding import PartitionSpec as P

RIM_ROWS = 3
F32, BF16 = jnp.float32, jnp.bfloat16


def split_two(weight):
    high = weight.astype(BF16)
    return high, (weight - high.astype(F32)).astype(BF16)


def block_diagonal(weight, channels):
    t, r = weight.shape
    eye = jnp.eye(channels, dtype=F32)
    return (eye[:, None, :, None] * weight[None, :, None, :]).reshape(channels * t, channels * r)


def mean_kernel(scale, x_ref, m_ref, high_ref, low_ref, out_ref):
    mean = (jnp.dot(x_ref[0], m_ref[...], preferred_element_type=F32) * scale).astype(BF16)
    out_ref[0] = jnp.dot(high_ref[...], mean, preferred_element_type=F32) + jnp.dot(
        low_ref[...], mean, preferred_element_type=F32
    )


def dates_kernel(bins_ref, p_ref, o_ref, clim_ref, out_ref):
    dates, leads = p_ref.shape[0], p_ref.shape[1]
    shape = p_ref.shape[3:]
    for lead in range(leads):

        def step(d, sums):
            c = clim_ref[bins_ref[d, lead], 0].astype(F32)
            p = p_ref[d, lead, 0].astype(F32)
            o = o_ref[d, lead, 0].astype(F32)
            e, f, t = p - o, p - c, o - c
            return (sums[0] + e * e, sums[1] + f * t, sums[2] + f * f, sums[3] + t * t)

        sums = lax.fori_loop(0, dates, step, (jnp.zeros(shape, F32),) * 4, unroll=4)
        for k in range(4):
            out_ref[lead, k, 0] = sums[k]


def body(sn, rows, extent, members, bins, prog, obs):
    slots, channels, band, q = sn.shape
    tile = rows.shape[0]
    dates, leads, _, _, j = prog.shape
    refine = q // j
    n_lat = lax.axis_size("lat")
    lat_index = lax.axis_index("lat")
    scale = 1.0 / refine
    matrix = (jnp.arange(q)[:, None] // refine == jnp.arange(j)[None, :]).astype(BF16)

    def average(x):
        y = lax.dot_general(x, matrix, (((3,), (0,)), ((), ())), preferred_element_type=F32)
        return (y * scale).astype(BF16)

    up = [(i, i + 1) for i in range(n_lat - 1)]
    down = [(b, a) for a, b in up]
    before = lax.ppermute(average(sn[:, :, band - RIM_ROWS :]), "lat", up)
    after = lax.ppermute(average(sn[:, :, :RIM_ROWS]), "lat", down)

    local = rows - (lat_index * band - RIM_ROWS)
    live = jnp.arange(rows.shape[1], dtype=jnp.int32)[None, :] < members[:, None]
    raw = jnp.where(live, extent, jnp.zeros_like(extent))
    weight = raw / jnp.sum(raw, axis=1, keepdims=True)
    positions = jnp.arange(band + 2 * RIM_ROWS, dtype=jnp.int32)
    dense = jnp.sum(
        weight[:, :, None] * (local[:, :, None] == positions[None, None, :]).astype(F32), axis=1
    )
    high, low = split_two(dense)
    inner = slice(RIM_ROWS, RIM_ROWS + band)
    high_in = block_diagonal(high[:, inner].astype(F32), channels).astype(BF16)
    low_in = block_diagonal(low[:, inner].astype(F32), channels).astype(BF16)

    flat = sn.reshape(slots, channels * band, q)
    whole = pl.BlockSpec(memory_space=pltpu.VMEM)
    partial = pl.pallas_call(
        functools.partial(mean_kernel, scale),
        grid=(slots,),
        in_specs=[
            pl.BlockSpec((1, channels * band, q), lambda s: (s, 0, 0)),
            whole,
            whole,
            whole,
        ],
        out_specs=pl.BlockSpec((1, channels * tile, j), lambda s: (s, 0, 0)),
        out_shape=jax.ShapeDtypeStruct((slots, channels * tile, j), F32),
        compiler_params=pltpu.CompilerParams(vmem_limit_bytes=40 << 20),
        cost_estimate=pl.CostEstimate(
            flops=2 * sn.size * j, bytes_accessed=2 * sn.size, transcendentals=0
        ),
    )(flat, matrix, high_in, low_in)
    partial = partial.reshape(slots, channels, tile, j)
    halo = jnp.concatenate([before, after], axis=2)
    rim = jnp.concatenate([dense[:, :RIM_ROWS], dense[:, RIM_ROWS + band :]], axis=1)
    rim_high, rim_low = split_two(rim)
    both = jnp.concatenate([rim_high, rim_low], axis=0)
    fix = lax.dot_general(halo, both, (((2,), (1,)), ((), ())), preferred_element_type=F32)
    fix = jnp.moveaxis(fix, 3, 2)
    climate = (partial + fix[:, :, :tile] + fix[:, :, tile:]).astype(BF16)
    table = lax.all_gather(climate, "slot", axis=0, tiled=True)

    totals = pl.pallas_call(
        dates_kernel,
        grid=(channels,),
        in_specs=[
            pl.BlockSpec(memory_space=pltpu.SMEM),
            pl.BlockSpec((dates, leads, 1, tile, j), lambda c: (0, 0, c, 0, 0)),
            pl.BlockSpec((dates, leads, 1, tile, j), lambda c: (0, 0, c, 0, 0)),
            pl.BlockSpec((table.shape[0], 1, tile, j), lambda c: (0, c, 0, 0)),
        ],
        out_specs=pl.BlockSpec((leads, 4, 1, tile, j), lambda c: (0, 0, c, 0, 0)),
        out_shape=jax.ShapeDtypeStruct((leads, 4, channels, tile, j), F32),
        compiler_params=pltpu.CompilerParams(vmem_limit_bytes=40 << 20),
    )(bins, prog, obs, table)
    sums = lax.psum_scatter(totals, "slot", scatter_dimension=0, tiled=True)

    parallels = tile * n_lat
    latitude = (jnp.arange(parallels, dtype=F32) + 0.5) * (math.pi / parallels) - 0.5 * math.pi
    cosine = jnp.cos(latitude)
    factor = lax.dynamic_slice_in_dim(cosine, lat_index * tile, tile, 0) / jnp.mean(cosine)
    days = dates * lax.axis_size("slot")
    rmse = jnp.sqrt(factor[None, None, :, None] * sums[:, 0] / days)
    acc = sums[:, 1] / jnp.sqrt(sums[:, 2] * sums[:, 3] + 1e-06)
    return rmse, acc


def solution(mesh):
    placed = (
        P("slot", None, "lat", None),
        P("lat", None),
        P("lat", None),
        P("lat"),
        P("slot", None),
        P("slot", None, None, "lat", None),
        P("slot", None, None, "lat", None),
    )
    return jax.shard_map(
        body,
        mesh=mesh,
        in_specs=placed,
        out_specs=(P("slot", None, "lat", None), P("slot", None, "lat", None)),
        check_vma=False,
    )
```

```python
import math
import functools

import jax
import jax.numpy as jnp
from jax import lax
from jax.experimental import pallas as pl
from jax.experimental.pallas import tpu as pltpu
from jax.sharding import PartitionSpec as P

RIM_ROWS = 3
F32, BF16 = jnp.float32, jnp.bfloat16


def split_two(weight):
    high = weight.astype(BF16)
    return high, (weight - high.astype(F32)).astype(BF16)


def block_diagonal(weight, channels):
    t, r = weight.shape
    eye = jnp.eye(channels, dtype=F32)
    return (eye[:, None, :, None] * weight[None, :, None, :]).reshape(channels * t, channels * r)


def mean_kernel(scale, x_ref, m_ref, high_ref, low_ref, *refs):
    out_ref = refs[-1]
    mean = (jnp.dot(x_ref[0], m_ref[...], preferred_element_type=F32) * scale).astype(BF16)
    out_ref[0] = jnp.dot(high_ref[...], mean, preferred_element_type=F32) + jnp.dot(
        low_ref[...], mean, preferred_element_type=F32
    )


def dates_kernel(bins_ref, order_ref, p_ref, o_ref, *refs):
    pieces, (keep_ref, send_ref, table) = refs[:-3], refs[-3:]
    dates, leads = p_ref.shape[0], p_ref.shape[1]
    shape = p_ref.shape[3:]
    at = 0
    for piece in pieces:
        table[at : at + piece.shape[0]] = piece[:, 0]
        at += piece.shape[0]
    half = leads // 2
    for place in range(leads):
        lead = order_ref[place]

        def step(d, sums):
            c = table[bins_ref[d, lead]]
            p = p_ref[d, lead, 0].astype(F32)
            o = o_ref[d, lead, 0].astype(F32)
            e, f, t = p - o, p - c, o - c
            return (sums[0] + e * e, sums[1] + f * t, sums[2] + f * f, sums[3] + t * t)

        sums = lax.fori_loop(0, dates, step, (jnp.zeros(shape, F32),) * 4, unroll=4)
        out_ref = keep_ref if place < half else send_ref
        for k in range(4):
            out_ref[place % half, k, 0] = sums[k]


def swapped(value, mask):
    n = lax.axis_size("slot")
    return lax.ppermute(value, "slot", [(i, i ^ mask) for i in range(n)])


def reversed_bits(n):
    bits = n.bit_length() - 1
    return [sum(((r >> k) & 1) << (bits - 1 - k) for k in range(bits)) for r in range(n)]


def body(sn, rows, extent, members, bins, prog, obs):
    slots, channels, band, q = sn.shape
    tile = rows.shape[0]
    dates, leads, _, _, j = prog.shape
    refine = q // j
    n_lat = lax.axis_size("lat")
    lat_index = lax.axis_index("lat")
    scale = 1.0 / refine
    matrix = (jnp.arange(q)[:, None] // refine == jnp.arange(j)[None, :]).astype(BF16)

    def average(x):
        y = lax.dot_general(x, matrix, (((3,), (0,)), ((), ())), preferred_element_type=F32)
        return (y * scale).astype(BF16)

    up = [(i, i + 1) for i in range(n_lat - 1)]
    down = [(b, a) for a, b in up]
    before = lax.ppermute(average(sn[:, :, band - RIM_ROWS :]), "lat", up)
    after = lax.ppermute(average(sn[:, :, :RIM_ROWS]), "lat", down)

    local = rows - (lat_index * band - RIM_ROWS)
    live = jnp.arange(rows.shape[1], dtype=jnp.int32)[None, :] < members[:, None]
    raw = jnp.where(live, extent, jnp.zeros_like(extent))
    weight = raw / jnp.sum(raw, axis=1, keepdims=True)
    positions = jnp.arange(band + 2 * RIM_ROWS, dtype=jnp.int32)
    dense = jnp.sum(
        weight[:, :, None] * (local[:, :, None] == positions[None, None, :]).astype(F32), axis=1
    )
    high, low = split_two(dense)
    inner = slice(RIM_ROWS, RIM_ROWS + band)
    high_in = block_diagonal(high[:, inner].astype(F32), channels).astype(BF16)
    low_in = block_diagonal(low[:, inner].astype(F32), channels).astype(BF16)

    flat = sn.reshape(slots, channels * band, q)
    whole = pl.BlockSpec(memory_space=pltpu.VMEM)
    rim = jnp.concatenate([dense[:, :RIM_ROWS], dense[:, RIM_ROWS + band :]], axis=1)
    rim_high, rim_low = split_two(rim)
    both = jnp.concatenate([rim_high, rim_low], axis=0)
    n_slot = lax.axis_size("slot")
    me = lax.axis_index("slot")
    quarter = slots // 4
    cuts = [(k * quarter, quarter) for k in range(4)]
    masks = [1 << k for k in reversed(range(n_slot.bit_length() - 1))]
    gathered = {r: [] for r in range(n_slot)}
    arrived, earlier = [], []
    for first, count in cuts:
        partial = pl.pallas_call(
            functools.partial(mean_kernel, scale),
            grid=(count,),
            in_specs=[
                pl.BlockSpec((1, channels * band, q), lambda s, first=first: (s + first, 0, 0)),
                whole,
                whole,
                whole,
            ]
            + [pl.BlockSpec(memory_space=pl.ANY)] * len(earlier),
            out_specs=pl.BlockSpec((1, channels * tile, j), lambda s: (s, 0, 0)),
            out_shape=jax.ShapeDtypeStruct((count, channels * tile, j), F32),
            compiler_params=pltpu.CompilerParams(vmem_limit_bytes=40 << 20),
            cost_estimate=pl.CostEstimate(
                flops=2 * sn.size * j * count // slots,
                bytes_accessed=2 * sn.size * count // slots,
                transcendentals=0,
            ),
        )(flat, matrix, high_in, low_in, *earlier)
        partial = partial.reshape(count, channels, tile, j)
        halo = jnp.concatenate([before[first : first + count], after[first : first + count]], axis=2)
        fix = lax.dot_general(halo, both, (((2,), (1,)), ((), ())), preferred_element_type=F32)
        fix = jnp.moveaxis(fix, 3, 2)
        climate = partial + fix[:, :, :tile] + fix[:, :, tile:]
        held = {0: climate}
        for mask in masks:
            held.update({r ^ mask: swapped(v, mask) for r, v in list(held.items())})
        arrived.append(held[masks[0]])
        earlier = [climate] + arrived[-2:-1]
        for r in range(n_slot):
            gathered[r].append(held[r])
    pieces = [piece for r in range(n_slot) for piece in gathered[r]]
    places = ((bins // slots) ^ me) * slots + bins % slots

    group = leads // n_slot
    order = jnp.concatenate(
        [(me ^ r) * group + jnp.arange(group, dtype=jnp.int32) for r in reversed_bits(n_slot)]
    ).astype(jnp.int32)
    part = channels // 2
    summed = []
    for first in (0, part):
        field = pl.BlockSpec((dates, leads, 1, tile, j), lambda c, first=first: (0, 0, c + first, 0, 0))
        result = jax.ShapeDtypeStruct((leads // 2, 4, part, tile, j), F32)
        keep, send = pl.pallas_call(
            dates_kernel,
            grid=(part,),
            in_specs=[
                pl.BlockSpec(memory_space=pltpu.SMEM),
                pl.BlockSpec(memory_space=pltpu.SMEM),
                field,
                field,
            ]
            + [
                pl.BlockSpec((v.shape[0], 1, tile, j), lambda c, first=first: (0, c + first, 0, 0))
                for v in pieces
            ],
            out_specs=[pl.BlockSpec((leads // 2, 4, 1, tile, j), lambda c: (0, 0, c, 0, 0))] * 2,
            out_shape=[result, result],
            scratch_shapes=[pltpu.VMEM((slots * n_slot, tile, j), F32)],
            compiler_params=pltpu.CompilerParams(vmem_limit_bytes=40 << 20),
            cost_estimate=pl.CostEstimate(
                flops=7 * prog.size, bytes_accessed=2 * prog.size, transcendentals=0
            ),
        )(places, order, prog, obs, *pieces)
        mask = 1
        while True:
            keep = keep + swapped(send, mask)
            mask *= 2
            if mask == n_slot:
                break
            middle = keep.shape[0] // 2
            keep, send = keep[:middle], keep[middle:]
        summed.append(keep)
    sums = jnp.concatenate(summed, axis=2)

    parallels = tile * n_lat
    latitude = (jnp.arange(parallels, dtype=F32) + 0.5) * (math.pi / parallels) - 0.5 * math.pi
    cosine = jnp.cos(latitude)
    factor = lax.dynamic_slice_in_dim(cosine, lat_index * tile, tile, 0) / jnp.mean(cosine)
    days = dates * lax.axis_size("slot")
    rmse = jnp.sqrt(factor[None, None, :, None] * sums[:, 0] / days)
    acc = sums[:, 1] / jnp.sqrt(sums[:, 2] * sums[:, 3] + 1e-06)
    return rmse, acc


def solution(mesh):
    placed = (
        P("slot", None, "lat", None),
        P("lat", None),
        P("lat", None),
        P("lat"),
        P("slot", None),
        P("slot", None, None, "lat", None),
        P("slot", None, None, "lat", None),
    )
    return jax.shard_map(
        body,
        mesh=mesh,
        in_specs=placed,
        out_specs=(P("slot", None, "lat", None), P("slot", None, "lat", None)),
        check_vma=False,
    )
```

```python
import math
import functools

import jax
import jax.numpy as jnp
from jax import lax
from jax.experimental import pallas as pl
from jax.experimental.pallas import tpu as pltpu
from jax.sharding import PartitionSpec as P

RIM_ROWS = 3
F32, BF16 = jnp.float32, jnp.bfloat16


def split_two(weight):
    high = weight.astype(BF16)
    return high, (weight - high.astype(F32)).astype(BF16)


def block_diagonal(weight, channels):
    t, r = weight.shape
    eye = jnp.eye(channels, dtype=F32)
    return (eye[:, None, :, None] * weight[None, :, None, :]).reshape(channels * t, channels * r)


def mean_kernel(scale, x_ref, m_ref, high_ref, low_ref, *refs):
    out_ref = refs[-1]
    slots, rows, q = x_ref.shape
    tall = out_ref.shape[1]

    def regrid(x, high, low):
        mean = (jnp.dot(x, m_ref[...], preferred_element_type=F32) * scale).astype(BF16)
        return jnp.dot(high, mean, preferred_element_type=F32) + jnp.dot(
            low, mean, preferred_element_type=F32
        )

    if rows % 16 == 0 and tall % 16 == 0:
        out = regrid(x_ref[...].reshape(slots * rows, q), high_ref[...], low_ref[...])
        for s in range(slots):
            out_ref[s] = out[s * tall : (s + 1) * tall]
    else:
        for s in range(slots):
            out_ref[s] = regrid(x_ref[s], high_ref[:tall, :rows], low_ref[:tall, :rows])


def dates_kernel(bins_ref, order_ref, p_ref, o_ref, *refs):
    pieces, (keep_ref, send_ref, table) = refs[:-3], refs[-3:]
    dates, leads = p_ref.shape[0], p_ref.shape[1]
    shape = p_ref.shape[3:]
    at = 0
    for piece in pieces:
        table[at : at + piece.shape[0]] = piece[:, 0]
        at += piece.shape[0]
    half = leads // 2
    for place in range(leads):
        lead = order_ref[place]

        def step(d, sums):
            c = table[bins_ref[d, lead]]
            p = p_ref[d, lead, 0].astype(F32)
            o = o_ref[d, lead, 0].astype(F32)
            e, f, t = p - o, p - c, o - c
            return (sums[0] + e * e, sums[1] + f * t, sums[2] + f * f, sums[3] + t * t)

        sums = lax.fori_loop(0, dates, step, (jnp.zeros(shape, F32),) * 4, unroll=4)
        out_ref = keep_ref if place < half else send_ref
        for k in range(4):
            out_ref[place % half, k, 0] = sums[k]


def swapped(value, mask):
    n = lax.axis_size("slot")
    return lax.ppermute(value, "slot", [(i, i ^ mask) for i in range(n)])


def reversed_bits(n):
    bits = n.bit_length() - 1
    return [sum(((r >> k) & 1) << (bits - 1 - k) for k in range(bits)) for r in range(n)]


def body(sn, rows, extent, members, bins, prog, obs):
    slots, channels, band, q = sn.shape
    tile = rows.shape[0]
    dates, leads, _, _, j = prog.shape
    refine = q // j
    n_lat = lax.axis_size("lat")
    lat_index = lax.axis_index("lat")
    scale = 1.0 / refine
    matrix = (jnp.arange(q)[:, None] // refine == jnp.arange(j)[None, :]).astype(BF16)

    def average(x):
        y = lax.dot_general(x, matrix, (((3,), (0,)), ((), ())), preferred_element_type=F32)
        return (y * scale).astype(BF16)

    up = [(i, i + 1) for i in range(n_lat - 1)]
    down = [(b, a) for a, b in up]
    before = lax.ppermute(average(sn[:, :, band - RIM_ROWS :]), "lat", up)
    after = lax.ppermute(average(sn[:, :, :RIM_ROWS]), "lat", down)

    local = rows - (lat_index * band - RIM_ROWS)
    live = jnp.arange(rows.shape[1], dtype=jnp.int32)[None, :] < members[:, None]
    raw = jnp.where(live, extent, jnp.zeros_like(extent))
    weight = raw / jnp.sum(raw, axis=1, keepdims=True)
    positions = jnp.arange(band + 2 * RIM_ROWS, dtype=jnp.int32)
    dense = jnp.sum(
        weight[:, :, None] * (local[:, :, None] == positions[None, None, :]).astype(F32), axis=1
    )
    high, low = split_two(dense)
    width, batch = channels // 4, slots // 4
    inner = slice(RIM_ROWS, RIM_ROWS + band)
    high_in = block_diagonal(high[:, inner].astype(F32), batch * width).astype(BF16)
    low_in = block_diagonal(low[:, inner].astype(F32), batch * width).astype(BF16)

    flat = sn.reshape(slots, channels * band, q)
    whole = pl.BlockSpec(memory_space=pltpu.VMEM)
    rim = jnp.concatenate([dense[:, :RIM_ROWS], dense[:, RIM_ROWS + band :]], axis=1)
    rim_high, rim_low = split_two(rim)
    both = jnp.concatenate([rim_high, rim_low], axis=0)
    n_slot = lax.axis_size("slot")
    me = lax.axis_index("slot")
    masks = [1 << k for k in reversed(range(n_slot.bit_length() - 1))]
    gathered = []
    arrived, earlier = [], []
    for first in range(0, channels, width):
        source, at = flat, first // width
        if (width * band) % 16:
            source, at = flat[:, first * band : (first + width) * band], 0
        partial = pl.pallas_call(
            functools.partial(mean_kernel, scale),
            grid=(slots // batch,),
            in_specs=[
                pl.BlockSpec(
                    (batch, width * band, q), lambda s, at=at: (s, at, 0)
                ),
                whole,
                whole,
                whole,
            ]
            + [pl.BlockSpec(memory_space=pl.ANY)] * len(earlier),
            out_specs=pl.BlockSpec((batch, width * tile, j), lambda s: (s, 0, 0)),
            out_shape=jax.ShapeDtypeStruct((slots, width * tile, j), F32),
            compiler_params=pltpu.CompilerParams(vmem_limit_bytes=40 << 20),
            cost_estimate=pl.CostEstimate(
                flops=2 * sn.size * j * width // channels,
                bytes_accessed=2 * sn.size * width // channels,
                transcendentals=0,
            ),
        )(source, matrix, high_in, low_in, *earlier)
        partial = partial.reshape(slots, width, tile, j)
        own = slice(first, first + width)
        halo = jnp.concatenate([before[:, own], after[:, own]], axis=2)
        fix = lax.dot_general(halo, both, (((2,), (1,)), ((), ())), preferred_element_type=F32)
        fix = jnp.moveaxis(fix, 3, 2)
        climate = partial + fix[:, :, :tile] + fix[:, :, tile:]
        held = {0: climate}
        for mask in masks:
            held.update({r ^ mask: swapped(v, mask) for r, v in list(held.items())})
        arrived.append(held[masks[0]])
        earlier = [climate] + arrived[-2:-1]
        gathered.append([held[r] for r in range(n_slot)])
    places = ((bins // slots) ^ me) * slots + bins % slots

    group = leads // n_slot
    order = jnp.concatenate(
        [(me ^ r) * group + jnp.arange(group, dtype=jnp.int32) for r in reversed_bits(n_slot)]
    ).astype(jnp.int32)
    summed = []
    for k, pieces in enumerate(gathered):
        first = k * width
        field = pl.BlockSpec((dates, leads, 1, tile, j), lambda c, first=first: (0, 0, c + first, 0, 0))
        result = jax.ShapeDtypeStruct((leads // 2, 4, width, tile, j), F32)
        keep, send = pl.pallas_call(
            dates_kernel,
            grid=(width,),
            in_specs=[
                pl.BlockSpec(memory_space=pltpu.SMEM),
                pl.BlockSpec(memory_space=pltpu.SMEM),
                field,
                field,
            ]
            + [
                pl.BlockSpec((v.shape[0], 1, tile, j), lambda c: (0, c, 0, 0))
                for v in pieces
            ],
            out_specs=[pl.BlockSpec((leads // 2, 4, 1, tile, j), lambda c: (0, 0, c, 0, 0))] * 2,
            out_shape=[result, result],
            scratch_shapes=[pltpu.VMEM((slots * n_slot, tile, j), F32)],
            compiler_params=pltpu.CompilerParams(vmem_limit_bytes=52 << 20),
            cost_estimate=pl.CostEstimate(
                flops=14 * prog.size // 4, bytes_accessed=prog.size, transcendentals=0
            ),
        )(places, order, prog, obs, *pieces)
        mask = 1
        while True:
            keep = keep + swapped(send, mask)
            mask *= 2
            if mask == n_slot:
                break
            middle = keep.shape[0] // 2
            keep, send = keep[:middle], keep[middle:]
        summed.append(keep)
    sums = jnp.concatenate(summed, axis=2)

    parallels = tile * n_lat
    latitude = (jnp.arange(parallels, dtype=F32) + 0.5) * (math.pi / parallels) - 0.5 * math.pi
    cosine = jnp.cos(latitude)
    factor = lax.dynamic_slice_in_dim(cosine, lat_index * tile, tile, 0) / jnp.mean(cosine)
    days = dates * lax.axis_size("slot")
    rmse = jnp.sqrt(factor[None, None, :, None] * sums[:, 0] / days)
    acc = sums[:, 1] / jnp.sqrt(sums[:, 2] * sums[:, 3] + 1e-06)
    return rmse, acc


def solution(mesh):
    placed = (
        P("slot", None, "lat", None),
        P("lat", None),
        P("lat", None),
        P("lat"),
        P("slot", None),
        P("slot", None, None, "lat", None),
        P("slot", None, None, "lat", None),
    )
    return jax.shard_map(
        body,
        mesh=mesh,
        in_specs=placed,
        out_specs=(P("slot", None, "lat", None), P("slot", None, "lat", None)),
        check_vma=False,
    )
```
